256 devices in a mesh: row: 8 (over x, core), col: 32 (over z, y).
Axes of the slice: x: 4, y: 4, z: 8, core: 2. Of those that a mesh axis runs over, the one named last changes fastest.
Arguments:
- right_sides: float32 [4, 8, 32, 128, 128], P(None, 'row', 'col'), may hold values from -6 to 6
- inverses: bfloat16 [4, 8, 32, 128, 128], P(None, 'row', 'col'), may hold values from -1 to 2, as said below
- blocks: bfloat16 [3, 8, 32, 2, 8, 6, 128, 128], P(None, 'row', 'col'), may hold values from -0.0546875 to 0.0546875
- sources: int32 [3, 8, 32, 2, 8, 6], P(None, 'row', 'col'), may hold values from 0 to 31
Outputs:
- solution: bfloat16 [4, 8, 32, 128, 128], P(None, 'row', 'col')
- back_solution: float32 [4, 8, 32, 128, 128], P(None, 'row', 'col')
The draws below stay inside these ranges and needn't reach their ends.
Inputs may be any that keep to these rules, and one draw needn't show every extreme that they name: `inverses`: each matrix is the inverse of one supernode's diagonal block.
All inputs are finite; a program needn't handle non-finite values.
Results may differ from the reference program's by a relative error of at most 0.03.
Values may be sent and summed in bfloat16 or wider, within the bound.
A program may use at most 64 MiB of HBM per device.

```python
import math
import jax
import jax.numpy as jnp
from jax import lax

B = 128
R = 128
LEV = 4
K = 6
N_ROW = 8
N_COL = 32


def draw_inverses(key, part):
    key = jax.random.fold_in(key, 7)
    first_key, second_key = jax.random.split(key)
    shape = (LEV, N_ROW, N_COL, B, B)
    spread = jax.random.truncated_normal(first_key, -4.0, 4.0, shape, jnp.float32) * (0.5 / math.sqrt(B))
    diagonal = jax.random.uniform(second_key, shape[:-1], jnp.float32, 0.6, 1.2)
    identity = jnp.eye(B, dtype=jnp.float32)
    return (spread + diagonal[..., None] * identity).astype(jnp.bfloat16)


def plant(entries, key, low, largest):
    dims = entries.shape
    place = [jax.random.randint(jax.random.fold_in(key, axis), (), 0, dims[axis]) for axis in range(len(dims))]
    entries = entries.at[tuple(place)].set(low)
    longest = dims.index(max(dims))
    place[longest] = (place[longest] + 1) % dims[longest]
    return entries.at[tuple(place)].set(largest)


def block_levels(rng, extent, pieces, smallest, top_value):
    level, own = 1.0, jax.random.fold_in(rng, 6)
    for dim, shards_of in pieces:
        draws = jnp.exp(jax.random.uniform(jax.random.fold_in(own, dim), (shards_of,), jnp.float32, smallest / len(pieces), top_value / len(pieces)))
        level = level * jnp.repeat(draws, extent[dim] // shards_of).reshape([-1 if axis == dim else 1 for axis in range(len(extent))])
    return level


def bell_draw(key, extent, width, limit, pieces=(), kind=jnp.bfloat16):
    result = jax.random.normal(key, extent, jnp.float32) * width
    if len(pieces) > 0:
        result = block_levels(key, extent, pieces, -0.22, 0.18) * result
    return jnp.clip(result, min=-limit, max=limit).astype(kind)


def setup_inputs(seed: int = 0) -> dict:
    key_list = jax.random.split(jax.random.key(seed), 5)
    return {
        "right_sides": bell_draw(key_list[0], (LEV, N_ROW, N_COL, B, R), 1.0, 6.0, ((1, 8), (2, 32)), jnp.float32),
        "inverses": draw_inverses(jax.random.fold_in(key_list[4], 71), 0),
        "blocks": bell_draw(key_list[2], (LEV - 1, N_ROW, N_COL, 2, N_ROW, K, B, B), (2 * K * N_ROW * B) ** -0.5, 0.0546875, ((1, 8), (2, 32))),
        "sources": plant(jax.random.randint(key_list[3], (LEV - 1, N_ROW, N_COL, 2, N_ROW, K), 0, N_COL), jax.random.fold_in(key_list[3], 1), 0, N_COL - 1).astype(jnp.int32),
    }


def forward_part(row_blocks, row_sources, solved, grid_rows, grid_cols):
    def one_row(running, element):
        part_blocks, part_sources, part_solved = element
        chosen = jnp.take(part_solved, part_sources, axis=0).astype(jnp.float32)
        product = jnp.einsum("ctkab,ctkbs->tcas", part_blocks.astype(jnp.float32), chosen,
                             precision=lax.Precision.HIGHEST)
        return running + product, None

    start = jnp.zeros((grid_rows, grid_cols, solved.shape[2], solved.shape[3]), jnp.float32)
    summed, _ = lax.scan(one_row, start, (row_blocks, row_sources, solved))
    return summed


def backward_part(row_blocks, row_sources, column_copy, grid_cols):
    copy_wide = column_copy.astype(jnp.float32)

    def one_row(element):
        part_blocks, part_sources = element
        products = jnp.einsum("ctkab,tcas->ctkbs", part_blocks.astype(jnp.float32), copy_wide,
                              precision=lax.Precision.HIGHEST)
        flattened = products.reshape((-1,) + products.shape[3:])
        return jax.ops.segment_sum(flattened, part_sources.reshape(-1).astype(jnp.int32),
                                   num_segments=grid_cols)

    return lax.map(one_row, (row_blocks, row_sources))


def reference(right_sides, inverses, blocks, sources):
    levels = right_sides.shape[0]
    summit = levels - 1
    grid_rows = right_sides.shape[1]
    grid_cols = right_sides.shape[2]
    empty_sums = jnp.zeros(right_sides.shape[1:], jnp.float32)
    updates = [empty_sums for height in range(levels)]
    solved_list = []
    for height in range(levels):
        forward_rhs = (right_sides[height] - updates[height]).astype(jnp.bfloat16)
        solved = jnp.einsum("rcab,rcbs->rcas", inverses[height].astype(jnp.float32),
                            forward_rhs.astype(jnp.float32),
                            precision=lax.Precision.HIGHEST).astype(jnp.bfloat16)
        solved_list.append(solved)
        if height < summit:
            for jump_index in range(2):
                target = min(height + 1 + jump_index, summit)
                updates[target] = updates[target] + forward_part(
                    blocks[height, :, :, jump_index], sources[height, :, :, jump_index],
                    solved, grid_rows, grid_cols)
    copies = [None] * levels
    back_values = [None] * levels
    for height in range(summit, -1, -1):
        if height == summit:
            back_update = empty_sums
        else:
            near_part = backward_part(blocks[height, :, :, 0], sources[height, :, :, 0],
                                      copies[height + 1], grid_cols)
            far_part = backward_part(blocks[height, :, :, 1], sources[height, :, :, 1],
                                     copies[min(height + 2, summit)], grid_cols)
            back_update = near_part + far_part
        back_rhs = (solved_list[height].astype(jnp.float32) - back_update).astype(jnp.bfloat16)
        back_value = jnp.einsum("rcba,rcbs->rcas", inverses[height].astype(jnp.float32),
                                back_rhs.astype(jnp.float32), precision=lax.Precision.HIGHEST)
        back_values[height] = back_value
        copies[height] = back_value.astype(jnp.bfloat16)
    return jnp.stack(solved_list), jnp.stack(back_values)
```

```python
import jax
import jax.numpy as jnp
from jax import lax
from jax.experimental import pallas as pl
from jax.experimental.pallas import tpu as pltpu
from jax.sharding import PartitionSpec as P

CHAINS = 2
MESH = pl.DeviceIdType.MESH
BF16 = jnp.bfloat16
F32 = jnp.float32
LEVELS = 4
LOWER = 3
ROWS = 8
COLS = 32
DEEP = 8
WIDE = 4
PER = 6
HALF = ROWS * PER
N = 128


def dot_nt(a, b):
    return lax.dot_general(a, b, (((1,), (1,)), ((), ())), preferred_element_type=F32)


def dot_nn(a, b):
    return jnp.dot(a, b, preferred_element_type=F32)


def kernel(span, slots, order, target, keep, last, has, rs_hbm, inv_hbm, blk_hbm, sol_out, back_out, *scratch):
    it = iter(scratch)
    chains = N // span
    rs, inv, rs_t, sol_t, back_t = [next(it) for _ in range(5)]
    blk = [next(it) for _ in range(LOWER)]

    def per_pair():
        return [[next(it) for _ in range(chains)] for _ in range(LOWER)]

    gathered, part_out, part_in, copies = per_pair(), per_pair(), per_pair(), per_pair()
    seg, ry, rz, s2, s3, fz, fy = [per_pair() for _ in range(7)]
    pending = [[next(it) for _ in range(chains)] for _ in range(2)]
    own_part, far_scan, near_scan = [[next(it) for _ in range(chains)] for _ in range(3)]
    in_sem, z_sem, f_sem, b_sem = [next(it) for _ in range(4)]

    r = lax.axis_index("row")
    c = lax.axis_index("col")
    z = lax.div(c, WIDE)
    y = lax.rem(c, WIDE)

    def z_peer(d):
        return (r, lax.rem(z + d, DEEP) * WIDE + y)

    def y_peer(d):
        return (r, z * WIDE + lax.rem(y + d, WIDE))

    def row_peer(d):
        return (lax.rem(r + d, ROWS), c)

    def send(src, dst, send_sem, recv_sem, device):
        pltpu.make_async_remote_copy(
            src_ref=src, dst_ref=dst, send_sem=send_sem, recv_sem=recv_sem,
            device_id=device, device_id_type=MESH,
        ).start()

    def wait_for(ref, sem):
        pltpu.make_async_copy(ref, ref, sem).wait()

    barrier = pltpu.get_barrier_semaphore()
    for d in range(1, DEEP):
        pl.semaphore_signal(barrier, inc=1, device_id=z_peer(d), device_id_type=MESH)
    for d in range(1, ROWS):
        pl.semaphore_signal(barrier, inc=1, device_id=row_peer(d), device_id_type=MESH)
    for d in range(1, WIDE):
        pl.semaphore_signal(barrier, inc=1, device_id=y_peer(d), device_id_type=MESH)

    loads = [
        pltpu.make_async_copy(rs_hbm, rs, in_sem.at[0]),
        pltpu.make_async_copy(inv_hbm, inv, in_sem.at[1]),
    ] + [pltpu.make_async_copy(blk_hbm.at[l], blk[l], in_sem.at[2 + l]) for l in range(LOWER)]
    for load in loads:
        load.start()
    loads[0].wait()
    for l in range(LEVELS):
        rs_t[l] = rs[l].T
    loads[1].wait()

    def part(ch):
        return pl.ds(ch * span, span)

    def solve(level, ch, rhs):
        solved = dot_nt(rhs.astype(BF16), inv[level]).astype(BF16)
        sol_t[level, part(ch)] = solved.astype(F32)
        return solved

    def spread_column(l, ch):
        buf = gathered[l][ch]
        k = l * chains + ch
        own = buf.at[y]
        for d in (2, 1, 3):
            send(own, buf.at[y], f_sem.at[k, 0], f_sem.at[k, 1], y_peer(d))
        for d in (4, 3, 5, 2, 6):
            send(own, buf.at[(DEEP - d) * WIDE + y], f_sem.at[k, 0], z_sem.at[k, DEEP - d - 2], z_peer(d))

    def relay_column(l, ch):
        buf = gathered[l][ch]
        k = l * chains + ch
        wait_for(buf.at[pl.ds(0, 3)], f_sem.at[k, 1])
        here = buf.at[pl.ds(0, WIDE)]
        send(here, buf.at[pl.ds(7 * WIDE, WIDE)], f_sem.at[k, 0], f_sem.at[k, 2], z_peer(1))
        send(here, buf.at[pl.ds(WIDE, WIDE)], f_sem.at[k, 0], f_sem.at[k, 2], z_peer(7))
        for zr in (2, 6, 3, 5, 4):
            wait_for(buf.at[pl.ds(0, 1)], z_sem.at[k, zr - 2])
            got = buf.at[zr * WIDE + y]
            for d in (2, 1, 3):
                send(got, got, f_sem.at[k, 0], f_sem.at[k, 2], y_peer(d))

    def forward_term(l, h, ch, t):
        base = (l * 2 + h) * HALF + t * PER
        buf = gathered[l][ch]
        xs = jnp.concatenate([buf[slots[base + i]] for i in range(PER)], axis=1)
        ws = jnp.concatenate([blk[l][h * HALF + t * PER + i] for i in range(PER)], axis=1)
        return dot_nt(xs, ws)

    def near_forward(l, ch):
        k = l * chains + ch
        wait_for(gathered[l][ch].at[pl.ds(0, 23)], f_sem.at[k, 2])

        def total(t):
            value = forward_term(l, 0, ch, t)
            if l == 2:
                value = value + forward_term(l, 1, ch, t)
            if l > 0:
                value = value + pending[l - 1][ch][t]
            return value

        def step(i, carry):
            d = 1 + lax.rem(i + 2, 7)
            t = lax.rem(r + d, ROWS)
            part_out[l][ch][t] = total(t).astype(BF16)
            send(part_out[l][ch].at[t], part_in[l][ch].at[d - 1], f_sem.at[k, 3], f_sem.at[k, 4], row_peer(d))
            return carry

        lax.fori_loop(0, 7, step, 0, unroll=True)
        own_part[ch][...] = total(r)

    def far_forward(l, ch):
        def step(t, carry):
            pending[l][ch][t] = forward_term(l, 1, ch, t)
            return carry

        lax.fori_loop(0, ROWS, step, 0, unroll=2)

    def spread_row(level, ch, value):
        buf = copies[level - 1][ch]
        k = (level - 1) * chains + ch
        buf[r] = value
        for d in (4, 5, 3, 2, 6, 7, 1):
            send(buf.at[r], buf.at[r], b_sem.at[k, 0], b_sem.at[k, 1], row_peer(d))

    def next_forward(level, ch):
        l = level - 1
        k = l * chains + ch
        wait_for(part_in[l][ch], f_sem.at[k, 4])
        update = own_part[ch][...]
        for i in range(7):
            update = update + part_in[l][ch][i].astype(F32)
        solved = solve(level, ch, rs_t[level, part(ch)] - update)
        if level < LOWER:
            gathered[level][ch][y] = solved
            spread_column(level, ch)
        else:
            back = dot_nn(solved, inv[level])
            back_t[level, part(ch)] = back
            spread_row(level, ch, back.astype(BF16))

    def scan(l, h, ch, buf, out):
        base = (l * 2 + h) * HALF

        def step(i, total):
            term = dot_nn(buf[target[base + i]], blk[l][order[base + i]])
            total = total * keep[base + i] + term
            out[i] = total
            return total

        lax.fori_loop(0, HALF, step, jnp.zeros((span, N), F32), unroll=8)

    def near_backward(l, ch):
        k = l * chains + ch
        level = l + 1
        buf = copies[l][ch]
        wait_for(buf.at[pl.ds(0, 7)], b_sem.at[k, 1])
        scan(l, 0, ch, buf, near_scan[ch])
        if l == 2:
            scan(l, 1, ch, buf, far_scan[ch])
        near, far = l * 2 * COLS, (l * 2 + 1) * COLS

        def step(i, carry):
            for w in range(WIDE):
                j = i * WIDE + w
                value = near_scan[ch][last[near + j]] * has[near + j]
                value = value + far_scan[ch][last[far + j]] * has[far + j]
                seg[l][ch][i, w] = value.astype(BF16)
            return carry

        lax.fori_loop(0, DEEP, step, 0, unroll=2)
        for d in (2, 1, 3):
            send(seg[l][ch].at[pl.ds(2, 5), lax.rem(y + d, WIDE)], ry[l][ch].at[d - 1],
                 b_sem.at[k, 2], b_sem.at[k, 3], y_peer(d))
        send(seg[l][ch].at[1], rz[l][ch].at[0], b_sem.at[k, 2], b_sem.at[k, 4], z_peer(1))
        send(seg[l][ch].at[7], rz[l][ch].at[1], b_sem.at[k, 2], b_sem.at[k, 4], z_peer(7))

    def far_backward(l, ch):
        scan(l, 1, ch, copies[l + 1][ch], far_scan[ch])

    def relay_backward(l, ch):
        k = l * chains + ch
        wait_for(ry[l][ch], b_sem.at[k, 3])
        for i in (2, 1, 3, 0, 4):
            value = seg[l][ch][i + 2, y].astype(F32)
            for d in range(3):
                value = value + ry[l][ch][d, i].astype(F32)
            s2[l][ch][i] = value.astype(BF16)
            send(s2[l][ch].at[i], fz[l][ch].at[i], b_sem.at[k, 2], b_sem.at[k, 5], z_peer(i + 2))
        wait_for(rz[l][ch], b_sem.at[k, 4])
        for d in (2, 1, 3):
            other = lax.rem(y + d, WIDE)
            value = seg[l][ch][0, other].astype(F32)
            for e in range(2):
                value = value + rz[l][ch][e, other].astype(F32)
            s3[l][ch][d - 1] = value.astype(BF16)
            send(s3[l][ch].at[d - 1], fy[l][ch].at[d - 1], b_sem.at[k, 2], b_sem.at[k, 6], y_peer(d))

    def next_backward(l, ch):
        k = l * chains + ch
        update = seg[l][ch][0, y].astype(F32)
        for e in range(2):
            update = update + rz[l][ch][e, y].astype(F32)
        wait_for(fy[l][ch], b_sem.at[k, 6])
        for i in range(3):
            update = update + fy[l][ch][i].astype(F32)
        wait_for(fz[l][ch], b_sem.at[k, 5])
        for i in range(5):
            update = update + fz[l][ch][i].astype(F32)
        rhs = (sol_t[l, part(ch)] - update).astype(BF16)
        back = dot_nn(rhs, inv[l])
        back_t[l, part(ch)] = back
        if l > 0:
            spread_row(l, ch, back.astype(BF16))

    def finish(level):
        back_out[level] = back_t[level].T

    for ch in range(chains):
        gathered[0][ch][y] = solve(0, ch, rs_t[0, part(ch)])
    pl.semaphore_wait(barrier, 17)
    for ch in range(chains):
        spread_column(0, ch)
    for l in range(LOWER):
        for ch in range(chains):
            relay_column(l, ch)
        loads[2 + l].wait()
        for ch in range(chains):
            near_forward(l, ch)
        for ch in range(chains):
            if l < 2:
                far_forward(l, ch)
            next_forward(l + 1, ch)
    for l in (2, 1, 0):
        for ch in range(chains):
            near_backward(l, ch)
        if l == 2:
            for level in range(LEVELS):
                sol_out[level] = sol_t[level].T.astype(BF16)
        else:
            finish(l + 2)
        for ch in range(chains):
            if l > 0:
                far_backward(l - 1, ch)
            relay_backward(l, ch)
        for ch in range(chains):
            next_backward(l, ch)
    finish(1)
    finish(0)
    for l in range(LOWER):
        for ch in range(chains):
            k = l * chains + ch
            wait_for(gathered[l][ch].at[pl.ds(0, 31)], f_sem.at[k, 0])
            wait_for(part_in[l][ch], f_sem.at[k, 3])
            wait_for(copies[l][ch].at[pl.ds(0, 7)], b_sem.at[k, 0])
            wait_for(gathered[l][ch].at[pl.ds(0, 31)], b_sem.at[k, 2])


def index_tables(sources, z):
    src = sources.reshape(LOWER * 2, HALF)
    slots = lax.rem(lax.div(src, WIDE) + DEEP - z, DEEP) * WIDE + lax.rem(src, WIDE)
    place = jnp.arange(HALF, dtype=jnp.int32)
    a, b = src[:, :, None], src[:, None, :]
    before = (b < a) | ((b == a) & (place[None, None, :] < place[None, :, None]))
    rank = jnp.sum(before.astype(jnp.int32), axis=2)
    pick = rank[:, None, :] == place[None, :, None]
    order = jnp.sum(jnp.where(pick, place[None, None, :], 0), axis=2)
    ordered = jnp.sum(jnp.where(pick, src[:, None, :], 0), axis=2)
    previous = jnp.concatenate([jnp.full((LOWER * 2, 1), -1, jnp.int32), ordered[:, :-1]], axis=1)
    keep = (ordered == previous).astype(F32)
    slot = jnp.arange(COLS, dtype=jnp.int32)
    column = lax.rem(lax.div(slot, WIDE) + z, DEEP) * WIDE + lax.rem(slot, WIDE)
    upto = jnp.sum((src[:, None, :] <= column[None, :, None]).astype(jnp.int32), axis=2)
    has = jnp.any(src[:, None, :] == column[None, :, None], axis=2).astype(F32)
    last = jnp.maximum(upto - 1, 0)
    shift = jnp.arange(LOWER * 2, dtype=jnp.int32)[:, None] % 2 * HALF
    return (slots.reshape(-1), (order + shift).reshape(-1), (order // PER).reshape(-1),
            keep.reshape(-1), last.reshape(-1), has.reshape(-1))


def body(right_sides, inverses, blocks, sources):
    chains = CHAINS
    span = N // chains
    z = lax.div(lax.axis_index("col"), WIDE)
    tables = index_tables(sources, z)

    def tile(*lead, dtype=BF16):
        return pltpu.VMEM((*lead, span, N), dtype)

    def per_pair(*lead):
        return [tile(*lead) for _ in range(LOWER * chains)]

    scratch = [
        pltpu.VMEM((LEVELS, N, N), F32),
        pltpu.VMEM((LEVELS, N, N), BF16),
        pltpu.VMEM((LEVELS, N, N), F32),
        pltpu.VMEM((LEVELS, N, N), F32),
        pltpu.VMEM((LEVELS, N, N), F32),
    ]
    scratch += [pltpu.VMEM((2 * HALF, N, N), BF16) for _ in range(LOWER)]
    scratch += per_pair(COLS) + per_pair(ROWS) + per_pair(ROWS - 1) + per_pair(ROWS)
    scratch += per_pair(DEEP, WIDE) + per_pair(3, 5) + per_pair(2, WIDE) + per_pair(5) + per_pair(3)
    scratch += per_pair(5) + per_pair(3)
    scratch += [tile(ROWS, dtype=F32) for _ in range(2 * chains)]
    scratch += [tile(dtype=F32) for _ in range(chains)]
    scratch += [tile(HALF, dtype=F32) for _ in range(2 * chains)]
    scratch += [
        pltpu.SemaphoreType.DMA((2 + LOWER,)),
        pltpu.SemaphoreType.DMA((LOWER * chains, 5)),
        pltpu.SemaphoreType.DMA((LOWER * chains, 5)),
        pltpu.SemaphoreType.DMA((LOWER * chains, 7)),
    ]
    smem = pl.BlockSpec(memory_space=pltpu.SMEM)
    vmem = pl.BlockSpec(memory_space=pltpu.VMEM)
    hbm = pl.BlockSpec(memory_space=pl.ANY)

    def run(*refs):
        kernel(span, *refs)

    solved, back = pl.pallas_call(
        run,
        out_shape=(
            jax.ShapeDtypeStruct((LEVELS, N, N), BF16),
            jax.ShapeDtypeStruct((LEVELS, N, N), F32),
        ),
        in_specs=[smem] * 6 + [hbm] * 3,
        out_specs=(vmem, vmem),
        scratch_shapes=scratch,
        compiler_params=pltpu.CompilerParams(
            collective_id=0, has_side_effects=True, vmem_limit_bytes=48 * 1024 * 1024
        ),
    )(*tables, right_sides[:, 0, 0], inverses[:, 0, 0],
      blocks[:, 0, 0].reshape(LOWER, 2 * HALF, N, N))
    return solved[:, None, None], back[:, None, None]


def solution(mesh):
    return jax.shard_map(
        body,
        mesh=mesh,
        in_specs=(
            P(None, "row", "col", None, None),
            P(None, "row", "col", None, None),
            P(None, "row", "col", None, None, None, None, None),
            P(None, "row", "col", None, None, None),
        ),
        out_specs=(P(None, "row", "col", None, None), P(None, "row", "col", None, None)),
        check_vma=False,
    )
```

```python
import functools

import jax
import jax.numpy as jnp
from jax import lax
from jax.experimental import pallas as pl
from jax.experimental.pallas import tpu as pltpu
from jax.sharding import PartitionSpec as P

CHAINS = 4
MESH = pl.DeviceIdType.MESH
BF16 = jnp.bfloat16
F32 = jnp.float32
LEVELS = 4
LOWER = 3
ROWS = 8
COLS = 32
DEEP = 8
WIDE = 4
PER = 6
HALF = ROWS * PER
N = 128


def dot_nt(a, b):
    return lax.dot_general(a, b, (((1,), (1,)), ((), ())), preferred_element_type=F32)


def dot_nn(a, b):
    return jnp.dot(a, b, preferred_element_type=F32)


def index_tables(src, z, int_table, float_table):
    lane8 = lax.broadcasted_iota(jnp.int32, (8, N), 1)
    row8 = lax.broadcasted_iota(jnp.int32, (8, N), 0)

    def place(t, wide):
        for i in range(PER):
            here = lane8 == t * PER + i
            for lh in range(LOWER * 2):
                wide = jnp.where(here & (row8 == lh), src[lh // 2, i, lh % 2, t], wide)
        return wide

    wide = lax.fori_loop(0, ROWS, place, jnp.zeros((8, N), jnp.int32))
    tall = jnp.concatenate([wide, jnp.zeros((N - 8, N), jnp.int32)], axis=0).T
    first = lax.broadcasted_iota(jnp.int32, (HALF, N), 0)
    second = lax.broadcasted_iota(jnp.int32, (HALF, N), 1)
    lane = lax.broadcasted_iota(jnp.int32, (1, N), 1)
    column = (((lane >> 2) + z) & (DEEP - 1)) * WIDE + (lane & (WIDE - 1))
    group = lax.div(first, PER)

    def down(mask, value):
        return jnp.sum(jnp.where(mask, value, 0), axis=0, keepdims=True)

    def inside(value, limit):
        return jnp.minimum(jnp.maximum(value, 0), limit)

    for lh in range(LOWER * 2):
        a = jnp.broadcast_to(tall[0:HALF, lh:lh + 1], (HALF, N))
        b = jnp.broadcast_to(wide[lh:lh + 1, :], (HALF, N))
        before = ((b < a) | ((b == a) & (second < first))) & (second < HALF)
        rank = jnp.sum(jnp.where(before, 1, 0), axis=1, keepdims=True)
        pick = jnp.broadcast_to(rank, (HALF, N)) == second
        ordered = down(pick, a)
        same = (ordered == pltpu.roll(ordered, 1, 1)) & (lane > 0)
        int_table[0, lh:lh + 1, :] = inside(down(pick, first), HALF - 1) + (lh % 2) * HALF
        int_table[1, lh:lh + 1, :] = inside(down(pick, group), ROWS - 1)
        int_table[2, lh:lh + 1, :] = inside(down(a <= column, 1) - 1, HALF - 1)
        float_table[0, lh:lh + 1, :] = jnp.where(same, 1.0, 0.0)
        float_table[1, lh:lh + 1, :] = jnp.where(down(a == column, 1) > 0, 1.0, 0.0)


def kernel(span, src, rs_hbm, inv_hbm, blk_hbm, sol_out, back_out,
           rs, inv, rs_t, sol_t, back_t, blk, gathered, part_out, part_in, copies, seg, ry, rz, s2, s3,
           fz, fy, pending, held, held_back, near_scan, far_scan,
           int_vec, float_vec, ints, floats, in_sem, z_sem, f_sem, b_sem):
    chains = N // span
    r = lax.axis_index("row")
    c = lax.axis_index("col")
    z = lax.div(c, WIDE)
    y = lax.rem(c, WIDE)

    def z_peer(d):
        return (r, lax.rem(z + d, DEEP) * WIDE + y)

    def y_peer(d):
        return (r, z * WIDE + lax.rem(y + d, WIDE))

    def row_peer(d):
        return (lax.rem(r + d, ROWS), c)

    def send(src, dst, send_sem, recv_sem, device):
        pltpu.make_async_remote_copy(
            src_ref=src, dst_ref=dst, send_sem=send_sem, recv_sem=recv_sem,
            device_id=device, device_id_type=MESH,
        ).start()

    def wait_for(ref, sem):
        pltpu.make_async_copy(ref, ref, sem).wait()

    def each(count, step):
        def run(i, carry):
            step(i)
            return carry

        lax.fori_loop(0, count, run, 0)

    barrier = pltpu.get_barrier_semaphore()
    for d in range(1, DEEP):
        pl.semaphore_signal(barrier, inc=1, device_id=z_peer(d), device_id_type=MESH)
    for d in range(1, ROWS):
        pl.semaphore_signal(barrier, inc=1, device_id=row_peer(d), device_id_type=MESH)
    for d in range(1, WIDE):
        pl.semaphore_signal(barrier, inc=1, device_id=y_peer(d), device_id_type=MESH)

    load_rs = pltpu.make_async_copy(rs_hbm, rs, in_sem.at[0])
    load_inv = pltpu.make_async_copy(inv_hbm, inv, in_sem.at[1])

    def load_blk(l):
        return pltpu.make_async_copy(blk_hbm.at[l], blk.at[l], in_sem.at[2 + l])

    load_rs.start()
    load_inv.start()
    for l in range(LOWER):
        load_blk(l).start()
    pending[0] = jnp.zeros((ROWS, N, N), F32)
    load_rs.wait()

    rs_t[0] = rs[0].T
    load_inv.wait()

    def part(ch):
        return pl.ds(pl.multiple_of(ch * span, span), span)

    def solve(level, ch, rhs):
        solved = dot_nt(rhs.astype(BF16), inv[level]).astype(BF16)
        sol_t[level, part(ch)] = solved.astype(F32)
        return solved

    def spread_column(l, ch):
        buf = gathered.at[l, ch]
        k = l * chains + ch
        own = buf.at[y]
        for d in (2, 1, 3):
            send(own, buf.at[y], f_sem.at[k, 0], f_sem.at[k, 1], y_peer(d))
        for d in (4, 3, 5, 2, 6):
            send(own, buf.at[(DEEP - d) * WIDE + y], f_sem.at[k, 0], z_sem.at[k, DEEP - d - 2], z_peer(d))

    def relay_column(l, ch):
        buf = gathered.at[l, ch]
        k = l * chains + ch
        wait_for(buf.at[pl.ds(0, 3)], f_sem.at[k, 1])
        here = buf.at[pl.ds(0, WIDE)]
        send(here, buf.at[pl.ds(7 * WIDE, WIDE)], f_sem.at[k, 0], f_sem.at[k, 2], z_peer(1))
        send(here, buf.at[pl.ds(WIDE, WIDE)], f_sem.at[k, 0], f_sem.at[k, 2], z_peer(7))
        for zr in (2, 6, 3, 5, 4):
            wait_for(buf.at[pl.ds(0, 1)], z_sem.at[k, zr - 2])
            got = buf.at[zr * WIDE + y]
            for d in (2, 1, 3):
                send(got, got, f_sem.at[k, 0], f_sem.at[k, 2], y_peer(d))

    def forward_term(l, h, rows, t):
        def slot(i):
            column = src[l, i, h, t]
            return (((column >> 2) + (DEEP - z)) & (DEEP - 1)) * WIDE + (column & (WIDE - 1))

        xs = jnp.concatenate([held[slot(i), rows] for i in range(PER)], axis=1)
        ws = jnp.concatenate([blk[l, h * HALF + t * PER + i] for i in range(PER)], axis=1)
        return dot_nt(xs, ws)

    def near_forward(l, ch):
        k = l * chains + ch
        wait_for(gathered.at[l, ch, pl.ds(0, 23)], f_sem.at[k, 2])
        held[:, part(ch)] = gathered[l, ch]

        @pl.when(l == 2)
        def _():
            def step(t, carry):
                pending[2, t, part(ch)] = pending[2, t, part(ch)] + forward_term(l, 1, part(ch), t)
                return carry

            lax.fori_loop(0, ROWS, step, 0, unroll=True)

        def step(t, carry):
            value = forward_term(l, 0, part(ch), t) + pending[l, t, part(ch)]
            part_out[l, ch, t] = value.astype(BF16)
            return carry

        lax.fori_loop(0, ROWS, step, 0, unroll=True)
        for d in (4, 5, 3, 2, 6, 7, 1):
            t = lax.rem(r + d, ROWS)
            send(part_out.at[l, ch, t], part_in.at[l, ch, d - 1], f_sem.at[k, 3], f_sem.at[k, 4], row_peer(d))

    def far_forward(l):
        def step(t, carry):
            pending[lax.rem(l + 1, LOWER), t] = forward_term(l, 1, slice(None), t)
            return carry

        lax.fori_loop(0, ROWS, step, 0, unroll=True)

    def spread_row(level, ch, value):
        below = lax.rem(level + 2, LOWER)
        buf = copies.at[below, ch]
        k = below * chains + ch
        copies[below, ch, r] = value
        for d in (4, 5, 3, 2, 6, 7, 1):
            send(buf.at[r], buf.at[r], b_sem.at[k, 0], b_sem.at[k, 1], row_peer(d))

    def next_forward(l, ch):
        k = l * chains + ch
        level = l + 1
        wait_for(part_in.at[l, ch], f_sem.at[k, 4])
        update = part_out[l, ch, r].astype(F32)
        for i in range(7):
            update = update + part_in[l, ch, i].astype(F32)
        solved = solve(level, ch, rs_t[level, part(ch)] - update)

        @pl.when(level < LOWER)
        def _():
            gathered[lax.rem(level, LOWER), ch, y] = solved
            spread_column(lax.rem(level, LOWER), ch)

        @pl.when(level == LOWER)
        def _():
            back = dot_nn(solved, inv[LOWER])
            back_t[LOWER, part(ch)] = back
            spread_row(LOWER, ch, back.astype(BF16))

    def scan(l, h, out, rows, count):
        lh = l * 2 + h

        def step(i, total):
            value = held_back[ints[1, lh, i], rows]
            total = total * floats[0, lh, i] + dot_nn(value, blk[l, ints[0, lh, i]])
            out[i, rows] = total
            return total

        lax.fori_loop(0, HALF, step, jnp.zeros((count, N), F32), unroll=True)

    def near_backward(l, ch):
        k = l * chains + ch
        wait_for(copies.at[l, ch, pl.ds(0, 7)], b_sem.at[k, 1])
        held_back[:, part(ch)] = copies[l, ch]

        @pl.when(l == 2)
        def _():
            scan(l, 1, far_scan, part(ch), span)

        scan(l, 0, near_scan, part(ch), span)
        near, far = l * 2, l * 2 + 1

        def step(i, carry):
            for w in range(WIDE):
                j = i * WIDE + w
                value = near_scan[ints[2, near, j], part(ch)] * floats[1, near, j]
                value = value + far_scan[ints[2, far, j], part(ch)] * floats[1, far, j]
                seg[l, ch, i, w] = value.astype(BF16)
            return carry

        lax.fori_loop(0, DEEP, step, 0, unroll=2)
        for d in (2, 1, 3):
            send(seg.at[l, ch, pl.ds(2, 5), lax.rem(y + d, WIDE)], ry.at[l, ch, d - 1],
                 b_sem.at[k, 2], b_sem.at[k, 3], y_peer(d))
        send(seg.at[l, ch, 1], rz.at[l, ch, 0], b_sem.at[k, 2], b_sem.at[k, 4], z_peer(1))
        send(seg.at[l, ch, 7], rz.at[l, ch, 1], b_sem.at[k, 2], b_sem.at[k, 4], z_peer(7))

    def relay_backward(l, ch):
        k = l * chains + ch
        wait_for(ry.at[l, ch], b_sem.at[k, 3])
        for i in (2, 1, 3, 0, 4):
            value = seg[l, ch, i + 2, y].astype(F32)
            for d in range(3):
                value = value + ry[l, ch, d, i].astype(F32)
            s2[l, ch, i] = value.astype(BF16)
            send(s2.at[l, ch, i], fz.at[l, ch, i], b_sem.at[k, 2], b_sem.at[k, 5], z_peer(i + 2))
        wait_for(rz.at[l, ch], b_sem.at[k, 4])
        for d in (2, 1, 3):
            other = lax.rem(y + d, WIDE)
            value = seg[l, ch, 0, other].astype(F32)
            for e in range(2):
                value = value + rz[l, ch, e, other].astype(F32)
            s3[l, ch, d - 1] = value.astype(BF16)
            send(s3.at[l, ch, d - 1], fy.at[l, ch, d - 1], b_sem.at[k, 2], b_sem.at[k, 6], y_peer(d))

    def next_backward(l, ch):
        k = l * chains + ch
        update = seg[l, ch, 0, y].astype(F32)
        for e in range(2):
            update = update + rz[l, ch, e, y].astype(F32)
        wait_for(fy.at[l, ch], b_sem.at[k, 6])
        for i in range(3):
            update = update + fy[l, ch, i].astype(F32)
        wait_for(fz.at[l, ch], b_sem.at[k, 5])
        for i in range(5):
            update = update + fz[l, ch, i].astype(F32)
        rhs = (sol_t[l, part(ch)] - update).astype(BF16)
        back = dot_nn(rhs, inv[l])
        back_t[l, part(ch)] = back

        @pl.when(l > 0)
        def _():
            spread_row(l, ch, back.astype(BF16))

    @functools.partial(each, chains)
    def _(ch):
        gathered[0, ch, y] = solve(0, ch, rs_t[0, part(ch)])

    pl.semaphore_wait(barrier, 17)
    each(chains, lambda ch: spread_column(0, ch))
    index_tables(src, z, int_vec, float_vec)
    move_ints = pltpu.make_async_copy(int_vec, ints, in_sem.at[2 + LOWER])
    move_floats = pltpu.make_async_copy(float_vec, floats, in_sem.at[3 + LOWER])
    move_ints.start()
    move_floats.start()

    @functools.partial(each, LOWER)
    def _(i):
        rs_t[i + 1] = rs[i + 1].T

    move_ints.wait()
    move_floats.wait()

    @functools.partial(each, LOWER)
    def _(l):
        each(chains, lambda ch: relay_column(l, ch))
        load_blk(l).wait()
        each(chains, lambda ch: near_forward(l, ch))

        @pl.when(l < 2)
        def _():
            far_forward(l)

        each(chains, lambda ch: next_forward(l, ch))

    @functools.partial(each, LOWER)
    def _(step):
        l = 2 - step
        each(chains, lambda ch: near_backward(l, ch))

        @pl.when(l > 0)
        def _():
            scan(lax.rem(l + 2, LOWER), 1, far_scan, slice(None), N)

        sol_out[l + 1] = sol_t[l + 1].T.astype(BF16)
        back_out[l + 1] = back_t[l + 1].T
        each(chains, lambda ch: relay_backward(l, ch))
        each(chains, lambda ch: next_backward(l, ch))

    sol_out[0] = sol_t[0].T.astype(BF16)
    back_out[0] = back_t[0].T

    @functools.partial(each, LOWER * chains)
    def _(k):
        l, ch = lax.div(k, chains), lax.rem(k, chains)
        wait_for(gathered.at[l, ch, pl.ds(0, 31)], f_sem.at[k, 0])
        wait_for(part_in.at[l, ch], f_sem.at[k, 3])
        wait_for(copies.at[l, ch, pl.ds(0, 7)], b_sem.at[k, 0])
        wait_for(gathered.at[l, ch, pl.ds(0, 31)], b_sem.at[k, 2])


def body(right_sides, inverses, blocks, sources):
    chains = CHAINS
    span = N // chains

    def tile(*lead):
        return pltpu.VMEM((LOWER, chains, *lead, span, N), BF16)

    def whole(*lead, dtype=F32):
        return pltpu.VMEM((*lead, N, N), dtype)

    scratch = [
        whole(LEVELS), whole(LEVELS, dtype=BF16), whole(LEVELS), whole(LEVELS), whole(LEVELS),
        whole(LOWER, 2 * HALF, dtype=BF16),
        tile(COLS), tile(ROWS), tile(ROWS - 1), tile(ROWS),
        tile(DEEP, WIDE), tile(3, 5), tile(2, WIDE), tile(5), tile(3), tile(5), tile(3),
        whole(LOWER, ROWS), whole(COLS, dtype=BF16), whole(ROWS, dtype=BF16), whole(HALF), whole(HALF),
        pltpu.VMEM((3, 8, N), jnp.int32), pltpu.VMEM((2, 8, N), F32),
        pltpu.SMEM((3, 8, N), jnp.int32), pltpu.SMEM((2, 8, N), F32),
        pltpu.SemaphoreType.DMA((4 + LOWER,)),
        pltpu.SemaphoreType.DMA((LOWER * chains, 5)),
        pltpu.SemaphoreType.DMA((LOWER * chains, 5)),
        pltpu.SemaphoreType.DMA((LOWER * chains, 7)),
    ]
    smem = pl.BlockSpec(memory_space=pltpu.SMEM)
    vmem = pl.BlockSpec(memory_space=pltpu.VMEM)
    hbm = pl.BlockSpec(memory_space=pl.ANY)

    def run(*refs):
        kernel(span, *refs)

    solved, back = pl.pallas_call(
        run,
        out_shape=(
            jax.ShapeDtypeStruct((LEVELS, N, N), BF16),
            jax.ShapeDtypeStruct((LEVELS, N, N), F32),
        ),
        in_specs=[smem] + [hbm] * 3,
        out_specs=(vmem, vmem),
        scratch_shapes=scratch,
        compiler_params=pltpu.CompilerParams(
            collective_id=0, has_side_effects=True, vmem_limit_bytes=60 * 1024 * 1024
        ),
    )(jnp.transpose(sources[:, 0, 0], (0, 3, 1, 2)), right_sides[:, 0, 0], inverses[:, 0, 0],
      blocks[:, 0, 0].reshape(LOWER, 2 * HALF, N, N))
    return solved[:, None, None], back[:, None, None]


def solution(mesh):
    return jax.shard_map(
        body,
        mesh=mesh,
        in_specs=(
            P(None, "row", "col", None, None),
            P(None, "row", "col", None, None),
            P(None, "row", "col", None, None, None, None, None),
            P(None, "row", "col", None, None, None),
        ),
        out_specs=(P(None, "row", "col", None, None), P(None, "row", "col", None, None)),
        check_vma=False,
    )
```

```python
import functools

import jax
import jax.numpy as jnp
from jax import lax
from jax.experimental import pallas as pl
from jax.experimental.pallas import tpu as pltpu
from jax.sharding import PartitionSpec as P

CHAINS = 4
MESH = pl.DeviceIdType.MESH
BF16 = jnp.bfloat16
F32 = jnp.float32
LEVELS = 4
LOWER = 3
ROWS = 8
COLS = 32
DEEP = 8
WIDE = 4
PER = 6
HALF = ROWS * PER
N = 128


def dot_nt(a, b):
    return lax.dot_general(a, b, (((1,), (1,)), ((), ())), preferred_element_type=F32)


def dot_nn(a, b):
    return jnp.dot(a, b, preferred_element_type=F32)


def index_tables(src, z, int_table, float_table):
    lane8 = lax.broadcasted_iota(jnp.int32, (8, N), 1)
    row8 = lax.broadcasted_iota(jnp.int32, (8, N), 0)

    def place(t, wide):
        for i in range(PER):
            here = lane8 == t * PER + i
            for lh in range(LOWER * 2):
                wide = jnp.where(here & (row8 == lh), src[lh // 2, i, lh % 2, t], wide)
        return wide

    wide = lax.fori_loop(0, ROWS, place, jnp.zeros((8, N), jnp.int32))
    tall = jnp.concatenate([wide, jnp.zeros((N - 8, N), jnp.int32)], axis=0).T
    first = lax.broadcasted_iota(jnp.int32, (HALF, N), 0)
    second = lax.broadcasted_iota(jnp.int32, (HALF, N), 1)
    lane = lax.broadcasted_iota(jnp.int32, (1, N), 1)
    column = (((lane >> 2) + z) & (DEEP - 1)) * WIDE + (lane & (WIDE - 1))
    group = lax.div(first, PER)

    def down(mask, value):
        return jnp.sum(jnp.where(mask, value, 0), axis=0, keepdims=True)

    def inside(value, limit):
        return jnp.minimum(jnp.maximum(value, 0), limit)

    for lh in range(LOWER * 2):
        a = jnp.broadcast_to(tall[0:HALF, lh:lh + 1], (HALF, N))
        b = jnp.broadcast_to(wide[lh:lh + 1, :], (HALF, N))
        before = ((b < a) | ((b == a) & (second < first))) & (second < HALF)
        rank = jnp.sum(jnp.where(before, 1, 0), axis=1, keepdims=True)
        pick = jnp.broadcast_to(rank, (HALF, N)) == second
        ordered = down(pick, a)
        same = (ordered == pltpu.roll(ordered, 1, 1)) & (lane > 0)
        int_table[0, lh:lh + 1, :] = inside(down(pick, first), HALF - 1) + (lh % 2) * HALF
        int_table[1, lh:lh + 1, :] = inside(down(pick, group), ROWS - 1)
        int_table[2, lh:lh + 1, :] = inside(down(a <= column, 1) - 1, HALF - 1)
        float_table[0, lh:lh + 1, :] = jnp.where(same, 1.0, 0.0)
        float_table[1, lh:lh + 1, :] = jnp.where(down(a == column, 1) > 0, 1.0, 0.0)


def kernel(span, src, rs_hbm, inv_hbm, blk_hbm, sol_out, back_out,
           rs, inv, rs_t, sol_t, back_t, blk, gathered, part_out, part_in, copies, seg, ry, rz, s2, s3,
           fz, fy, pending, held, held_back, near_scan, far_scan,
           int_vec, float_vec, ints, floats, in_sem, z_sem, f_sem, b_sem):
    chains = N // span
    r = lax.axis_index("row")
    c = lax.axis_index("col")
    z = lax.div(c, WIDE)
    y = lax.rem(c, WIDE)

    def z_peer(d):
        return (r, lax.rem(z + d, DEEP) * WIDE + y)

    def y_peer(d):
        return (r, z * WIDE + lax.rem(y + d, WIDE))

    def row_peer(d):
        return (lax.rem(r + d, ROWS), c)

    def send(src, dst, send_sem, recv_sem, device):
        pltpu.make_async_remote_copy(
            src_ref=src, dst_ref=dst, send_sem=send_sem, recv_sem=recv_sem,
            device_id=device, device_id_type=MESH,
        ).start()

    def wait_for(ref, sem):
        pltpu.make_async_copy(ref, ref, sem).wait()

    def each(count, step, start=0):
        def run(i, carry):
            step(i)
            return carry

        lax.fori_loop(start, count, run, 0)

    half = chains // 2

    def early(step):
        each(half, step)

    def late(step):
        each(chains, step, half)

    early_rows = pl.ds(0, half * span)
    late_rows = pl.ds(half * span, half * span)

    barrier = pltpu.get_barrier_semaphore()
    for d in range(1, DEEP):
        pl.semaphore_signal(barrier, inc=1, device_id=z_peer(d), device_id_type=MESH)
    for d in range(1, ROWS):
        pl.semaphore_signal(barrier, inc=1, device_id=row_peer(d), device_id_type=MESH)
    for d in range(1, WIDE):
        pl.semaphore_signal(barrier, inc=1, device_id=y_peer(d), device_id_type=MESH)

    load_rs = pltpu.make_async_copy(rs_hbm, rs, in_sem.at[0])
    load_inv = pltpu.make_async_copy(inv_hbm, inv, in_sem.at[1])

    def load_blk(l):
        return pltpu.make_async_copy(blk_hbm.at[l], blk.at[l], in_sem.at[2 + l])

    load_rs.start()
    load_inv.start()
    for l in range(LOWER):
        load_blk(l).start()
    pending[0] = jnp.zeros((ROWS, N, N), F32)
    load_rs.wait()

    rs_t[0] = rs[0].T
    load_inv.wait()

    def part(ch):
        return pl.ds(pl.multiple_of(ch * span, span), span)

    def solve(level, ch, rhs):
        solved = dot_nt(rhs.astype(BF16), inv[level]).astype(BF16)
        sol_t[level, part(ch)] = solved.astype(F32)
        return solved

    def spread_column(l, ch):
        buf = gathered.at[l, ch]
        k = l * chains + ch
        own = buf.at[y]
        for d in (2, 1, 3):
            send(own, buf.at[y], f_sem.at[k, 0], f_sem.at[k, 1], y_peer(d))
        for d in (4, 3, 5, 2, 6):
            send(own, buf.at[(DEEP - d) * WIDE + y], f_sem.at[k, 0], z_sem.at[k, DEEP - d - 2], z_peer(d))

    def relay_column(l, ch):
        buf = gathered.at[l, ch]
        k = l * chains + ch
        wait_for(buf.at[pl.ds(0, 3)], f_sem.at[k, 1])
        here = buf.at[pl.ds(0, WIDE)]
        send(here, buf.at[pl.ds(7 * WIDE, WIDE)], f_sem.at[k, 0], f_sem.at[k, 2], z_peer(1))
        send(here, buf.at[pl.ds(WIDE, WIDE)], f_sem.at[k, 0], f_sem.at[k, 2], z_peer(7))
        for zr in (2, 6, 3, 5, 4):
            wait_for(buf.at[pl.ds(0, 1)], z_sem.at[k, zr - 2])
            got = buf.at[zr * WIDE + y]
            for d in (2, 1, 3):
                send(got, got, f_sem.at[k, 0], f_sem.at[k, 2], y_peer(d))

    def forward_term(l, h, rows, t):
        def slot(i):
            column = src[l, i, h, t]
            return (((column >> 2) + (DEEP - z)) & (DEEP - 1)) * WIDE + (column & (WIDE - 1))

        xs = jnp.concatenate([held[slot(i), rows] for i in range(PER)], axis=1)
        ws = jnp.concatenate([blk[l, h * HALF + t * PER + i] for i in range(PER)], axis=1)
        return dot_nt(xs, ws)

    def near_forward(l, ch):
        k = l * chains + ch
        wait_for(gathered.at[l, ch, pl.ds(0, 23)], f_sem.at[k, 2])
        held[:, part(ch)] = gathered[l, ch]

        @pl.when(l == 2)
        def _():
            def step(t, carry):
                pending[2, t, part(ch)] = pending[2, t, part(ch)] + forward_term(l, 1, part(ch), t)
                return carry

            lax.fori_loop(0, ROWS, step, 0, unroll=True)

        def step(t, carry):
            value = forward_term(l, 0, part(ch), t) + pending[l, t, part(ch)]
            part_out[l, ch, t] = value.astype(BF16)
            return carry

        lax.fori_loop(0, ROWS, step, 0, unroll=True)
        for d in (4, 5, 3, 2, 6, 7, 1):
            t = lax.rem(r + d, ROWS)
            send(part_out.at[l, ch, t], part_in.at[l, ch, d - 1], f_sem.at[k, 3], f_sem.at[k, 4], row_peer(d))

    def far_forward(l, rows):
        @pl.when(l < 2)
        def _():
            def step(t, carry):
                pending[lax.rem(l + 1, LOWER), t, rows] = forward_term(l, 1, rows, t)
                return carry

            lax.fori_loop(0, ROWS, step, 0, unroll=True)

    def spread_row(level, ch, value):
        below = lax.rem(level + 2, LOWER)
        buf = copies.at[below, ch]
        k = below * chains + ch
        copies[below, ch, r] = value
        for d in (4, 5, 3, 2, 6, 7, 1):
            send(buf.at[r], buf.at[r], b_sem.at[k, 0], b_sem.at[k, 1], row_peer(d))

    def next_forward(l, ch):
        k = l * chains + ch
        level = l + 1
        wait_for(part_in.at[l, ch], f_sem.at[k, 4])
        update = part_out[l, ch, r].astype(F32)
        for i in range(7):
            update = update + part_in[l, ch, i].astype(F32)
        solved = solve(level, ch, rs_t[level, part(ch)] - update)

        @pl.when(level < LOWER)
        def _():
            gathered[lax.rem(level, LOWER), ch, y] = solved
            spread_column(lax.rem(level, LOWER), ch)

        @pl.when(level == LOWER)
        def _():
            back = dot_nn(solved, inv[LOWER])
            back_t[LOWER, part(ch)] = back
            spread_row(LOWER, ch, back.astype(BF16))

    def scan(l, h, out, rows, count):
        lh = l * 2 + h

        def step(i, total):
            value = held_back[ints[1, lh, i], rows]
            total = total * floats[0, lh, i] + dot_nn(value, blk[l, ints[0, lh, i]])
            out[i, rows] = total
            return total

        lax.fori_loop(0, HALF, step, jnp.zeros((count, N), F32), unroll=True)

    def near_backward(l, ch):
        k = l * chains + ch
        wait_for(copies.at[l, ch, pl.ds(0, 7)], b_sem.at[k, 1])
        held_back[:, part(ch)] = copies[l, ch]

        @pl.when(l == 2)
        def _():
            scan(l, 1, far_scan, part(ch), span)

        scan(l, 0, near_scan, part(ch), span)
        near, far = l * 2, l * 2 + 1

        def step(i, carry):
            for w in range(WIDE):
                j = i * WIDE + w
                value = near_scan[ints[2, near, j], part(ch)] * floats[1, near, j]
                value = value + far_scan[ints[2, far, j], part(ch)] * floats[1, far, j]
                seg[l, ch, i, w] = value.astype(BF16)
            return carry

        lax.fori_loop(0, DEEP, step, 0, unroll=2)
        for d in (2, 1, 3):
            send(seg.at[l, ch, pl.ds(2, 5), lax.rem(y + d, WIDE)], ry.at[l, ch, d - 1],
                 b_sem.at[k, 2], b_sem.at[k, 3], y_peer(d))
        send(seg.at[l, ch, 1], rz.at[l, ch, 0], b_sem.at[k, 2], b_sem.at[k, 4], z_peer(1))
        send(seg.at[l, ch, 7], rz.at[l, ch, 1], b_sem.at[k, 2], b_sem.at[k, 4], z_peer(7))

    def relay_backward(l, ch):
        k = l * chains + ch
        wait_for(ry.at[l, ch], b_sem.at[k, 3])
        for i in (2, 1, 3, 0, 4):
            value = seg[l, ch, i + 2, y].astype(F32)
            for d in range(3):
                value = value + ry[l, ch, d, i].astype(F32)
            s2[l, ch, i] = value.astype(BF16)
            send(s2.at[l, ch, i], fz.at[l, ch, i], b_sem.at[k, 2], b_sem.at[k, 5], z_peer(i + 2))
        wait_for(rz.at[l, ch], b_sem.at[k, 4])
        for d in (2, 1, 3):
            other = lax.rem(y + d, WIDE)
            value = seg[l, ch, 0, other].astype(F32)
            for e in range(2):
                value = value + rz[l, ch, e, other].astype(F32)
            s3[l, ch, d - 1] = value.astype(BF16)
            send(s3.at[l, ch, d - 1], fy.at[l, ch, d - 1], b_sem.at[k, 2], b_sem.at[k, 6], y_peer(d))

    def next_backward(l, ch):
        k = l * chains + ch
        update = seg[l, ch, 0, y].astype(F32)
        for e in range(2):
            update = update + rz[l, ch, e, y].astype(F32)
        wait_for(fy.at[l, ch], b_sem.at[k, 6])
        for i in range(3):
            update = update + fy[l, ch, i].astype(F32)
        wait_for(fz.at[l, ch], b_sem.at[k, 5])
        for i in range(5):
            update = update + fz[l, ch, i].astype(F32)
        rhs = (sol_t[l, part(ch)] - update).astype(BF16)
        back = dot_nn(rhs, inv[l])
        back_t[l, part(ch)] = back

        @pl.when(l > 0)
        def _():
            spread_row(l, ch, back.astype(BF16))

    @functools.partial(each, chains)
    def _(ch):
        gathered[0, ch, y] = solve(0, ch, rs_t[0, part(ch)])

    pl.semaphore_wait(barrier, 17)
    early(lambda ch: spread_column(0, ch))
    index_tables(src, z, int_vec, float_vec)
    move_ints = pltpu.make_async_copy(int_vec, ints, in_sem.at[2 + LOWER])
    move_floats = pltpu.make_async_copy(float_vec, floats, in_sem.at[3 + LOWER])
    move_ints.start()
    move_floats.start()

    @functools.partial(each, LOWER)
    def _(i):
        rs_t[i + 1] = rs[i + 1].T

    move_ints.wait()
    move_floats.wait()

    def far_backward(l, rows):
        @pl.when(l > 0)
        def _():
            scan(lax.rem(l + 2, LOWER), 1, far_scan, rows, half * span)

    @functools.partial(each, LOWER)
    def _(l):
        early(lambda ch: relay_column(l, ch))

        @pl.when(l == 0)
        def _():
            late(lambda ch: spread_column(0, ch))

        @pl.when(l > 0)
        def _():
            late(lambda ch: next_forward(lax.rem(l + 2, LOWER), ch))

        load_blk(l).wait()
        early(lambda ch: near_forward(l, ch))
        late(lambda ch: relay_column(l, ch))
        far_forward(l, early_rows)
        early(lambda ch: next_forward(l, ch))
        late(lambda ch: near_forward(l, ch))
        far_forward(l, late_rows)

    @functools.partial(each, LOWER)
    def _(step):
        l = 2 - step
        early(lambda ch: near_backward(l, ch))

        @pl.when(l == 2)
        def _():
            late(lambda ch: next_forward(2, ch))

        @pl.when(l < 2)
        def _():
            late(lambda ch: next_backward(lax.rem(l + 1, LOWER), ch))

        early(lambda ch: relay_backward(l, ch))
        late(lambda ch: near_backward(l, ch))
        far_backward(l, early_rows)
        early(lambda ch: next_backward(l, ch))
        late(lambda ch: relay_backward(l, ch))
        far_backward(l, late_rows)
        sol_out[l + 1] = sol_t[l + 1].T.astype(BF16)
        back_out[l + 1] = back_t[l + 1].T

    late(lambda ch: next_backward(0, ch))
    sol_out[0] = sol_t[0].T.astype(BF16)
    back_out[0] = back_t[0].T

    @functools.partial(each, LOWER * chains)
    def _(k):
        l, ch = lax.div(k, chains), lax.rem(k, chains)
        wait_for(gathered.at[l, ch, pl.ds(0, 31)], f_sem.at[k, 0])
        wait_for(part_in.at[l, ch], f_sem.at[k, 3])
        wait_for(copies.at[l, ch, pl.ds(0, 7)], b_sem.at[k, 0])
        wait_for(gathered.at[l, ch, pl.ds(0, 31)], b_sem.at[k, 2])


def body(right_sides, inverses, blocks, sources):
    chains = CHAINS
    span = N // chains

    def tile(*lead):
        return pltpu.VMEM((LOWER, chains, *lead, span, N), BF16)

    def whole(*lead, dtype=F32):
        return pltpu.VMEM((*lead, N, N), dtype)

    scratch = [
        whole(LEVELS), whole(LEVELS, dtype=BF16), whole(LEVELS), whole(LEVELS), whole(LEVELS),
        whole(LOWER, 2 * HALF, dtype=BF16),
        tile(COLS), tile(ROWS), tile(ROWS - 1), tile(ROWS),
        tile(DEEP, WIDE), tile(3, 5), tile(2, WIDE), tile(5), tile(3), tile(5), tile(3),
        whole(LOWER, ROWS), whole(COLS, dtype=BF16), whole(ROWS, dtype=BF16), whole(HALF), whole(HALF),
        pltpu.VMEM((3, 8, N), jnp.int32), pltpu.VMEM((2, 8, N), F32),
        pltpu.SMEM((3, 8, N), jnp.int32), pltpu.SMEM((2, 8, N), F32),
        pltpu.SemaphoreType.DMA((4 + LOWER,)),
        pltpu.SemaphoreType.DMA((LOWER * chains, 5)),
        pltpu.SemaphoreType.DMA((LOWER * chains, 5)),
        pltpu.SemaphoreType.DMA((LOWER * chains, 7)),
    ]
    smem = pl.BlockSpec(memory_space=pltpu.SMEM)
    vmem = pl.BlockSpec(memory_space=pltpu.VMEM)
    hbm = pl.BlockSpec(memory_space=pl.ANY)

    def run(*refs):
        kernel(span, *refs)

    solved, back = pl.pallas_call(
        run,
        out_shape=(
            jax.ShapeDtypeStruct((LEVELS, N, N), BF16),
            jax.ShapeDtypeStruct((LEVELS, N, N), F32),
        ),
        in_specs=[smem] + [hbm] * 3,
        out_specs=(vmem, vmem),
        scratch_shapes=scratch,
        compiler_params=pltpu.CompilerParams(
            collective_id=0, has_side_effects=True, vmem_limit_bytes=60 * 1024 * 1024
        ),
    )(jnp.transpose(sources[:, 0, 0], (0, 3, 1, 2)), right_sides[:, 0, 0], inverses[:, 0, 0],
      blocks[:, 0, 0].reshape(LOWER, 2 * HALF, N, N))
    return solved[:, None, None], back[:, None, None]


def solution(mesh):
    return jax.shard_map(
        body,
        mesh=mesh,
        in_specs=(
            P(None, "row", "col", None, None),
            P(None, "row", "col", None, None),
            P(None, "row", "col", None, None, None, None, None),
            P(None, "row", "col", None, None, None),
        ),
        out_specs=(P(None, "row", "col", None, None), P(None, "row", "col", None, None)),
        check_vma=False,
    )
```

```python
import functools

import jax
import jax.numpy as jnp
from jax import lax
from jax.experimental import pallas as pl
from jax.experimental.pallas import tpu as pltpu
from jax.sharding import PartitionSpec as P

CHAINS = 4
MESH = pl.DeviceIdType.MESH
BF16 = jnp.bfloat16
F32 = jnp.float32
LEVELS = 4
LOWER = 3
ROWS = 8
COLS = 32
DEEP = 8
WIDE = 4
PER = 6
HALF = ROWS * PER
N = 128


def dot_nt(a, b):
    return lax.dot_general(a, b, (((1,), (1,)), ((), ())), preferred_element_type=F32)


def dot_nn(a, b):
    return jnp.dot(a, b, preferred_element_type=F32)


def index_tables(src, z, int_table, float_table):
    lane8 = lax.broadcasted_iota(jnp.int32, (8, N), 1)
    row8 = lax.broadcasted_iota(jnp.int32, (8, N), 0)

    def place(t, wide):
        for i in range(PER):
            here = lane8 == t * PER + i
            for lh in range(LOWER * 2):
                wide = jnp.where(here & (row8 == lh), src[lh // 2, i, lh % 2, t], wide)
        return wide

    wide = lax.fori_loop(0, ROWS, place, jnp.zeros((8, N), jnp.int32))
    tall = jnp.concatenate([wide, jnp.zeros((N - 8, N), jnp.int32)], axis=0).T
    first = lax.broadcasted_iota(jnp.int32, (HALF, N), 0)
    second = lax.broadcasted_iota(jnp.int32, (HALF, N), 1)
    lane = lax.broadcasted_iota(jnp.int32, (1, N), 1)
    column = (((lane >> 2) + z) & (DEEP - 1)) * WIDE + (lane & (WIDE - 1))
    group = lax.div(first, PER)

    def down(mask, value):
        return jnp.sum(jnp.where(mask, value, 0), axis=0, keepdims=True)

    def inside(value, limit):
        return jnp.minimum(jnp.maximum(value, 0), limit)

    for lh in range(LOWER * 2):
        a = jnp.broadcast_to(tall[0:HALF, lh:lh + 1], (HALF, N))
        b = jnp.broadcast_to(wide[lh:lh + 1, :], (HALF, N))
        before = ((b < a) | ((b == a) & (second < first))) & (second < HALF)
        rank = jnp.sum(jnp.where(before, 1, 0), axis=1, keepdims=True)
        pick = jnp.broadcast_to(rank, (HALF, N)) == second
        ordered = down(pick, a)
        same = (ordered == pltpu.roll(ordered, 1, 1)) & (lane > 0)
        int_table[0, lh:lh + 1, :] = inside(down(pick, first), HALF - 1) + (lh % 2) * HALF
        int_table[1, lh:lh + 1, :] = inside(down(pick, group), ROWS - 1)
        int_table[2, lh:lh + 1, :] = inside(down(a <= column, 1) - 1, HALF - 1)
        float_table[0, lh:lh + 1, :] = jnp.where(same, 1.0, 0.0)
        float_table[1, lh:lh + 1, :] = jnp.where(down(a == column, 1) > 0, 1.0, 0.0)


def kernel(span, src, rs_hbm, inv_hbm, blk_hbm, sol_t, back_t,
           rs, inv, rs_t, blk, gathered, part_out, part_in, copies, seg, ry, rz, s2, s3,
           fz, fy, pending, held, held_back, near_scan, far_scan,
           int_vec, float_vec, ints, floats, in_sem, z_sem, f_sem, b_sem):
    chains = N // span
    r = lax.axis_index("row")
    c = lax.axis_index("col")
    z = lax.div(c, WIDE)
    y = lax.rem(c, WIDE)

    def z_peer(d):
        return (r, lax.rem(z + d, DEEP) * WIDE + y)

    def y_peer(d):
        return (r, z * WIDE + lax.rem(y + d, WIDE))

    def row_peer(d):
        return (lax.rem(r + d, ROWS), c)

    def send(src, dst, send_sem, recv_sem, device):
        pltpu.make_async_remote_copy(
            src_ref=src, dst_ref=dst, send_sem=send_sem, recv_sem=recv_sem,
            device_id=device, device_id_type=MESH,
        ).start()

    def wait_for(ref, sem):
        pltpu.make_async_copy(ref, ref, sem).wait()

    def each(count, step, start=0):
        def run(i, carry):
            step(i)
            return carry

        lax.fori_loop(start, count, run, 0)

    half = chains // 2

    def early(step):
        each(half, step)

    def late(step):
        each(chains, step, half)

    early_rows = pl.ds(0, half * span)
    late_rows = pl.ds(half * span, half * span)

    barrier = pltpu.get_barrier_semaphore()
    for d in range(1, DEEP):
        pl.semaphore_signal(barrier, inc=1, device_id=z_peer(d), device_id_type=MESH)
    for d in range(1, ROWS):
        pl.semaphore_signal(barrier, inc=1, device_id=row_peer(d), device_id_type=MESH)
    for d in range(1, WIDE):
        pl.semaphore_signal(barrier, inc=1, device_id=y_peer(d), device_id_type=MESH)

    load_rs = pltpu.make_async_copy(rs_hbm, rs, in_sem.at[0])
    load_inv = pltpu.make_async_copy(inv_hbm, inv, in_sem.at[1])

    def load_blk(l):
        return pltpu.make_async_copy(blk_hbm.at[l], blk.at[l], in_sem.at[2 + l])

    load_rs.start()
    load_inv.start()
    for l in range(LOWER):
        load_blk(l).start()
    pending[0] = jnp.zeros((ROWS, N, N), F32)
    load_rs.wait()

    rs_t[0] = rs[0].T
    load_inv.wait()

    def part(ch):
        return pl.ds(pl.multiple_of(ch * span, span), span)

    def solve(level, ch, rhs):
        solved = dot_nt(rhs.astype(BF16), inv[level]).astype(BF16)
        sol_t[level, part(ch)] = solved.astype(F32)
        return solved

    def spread_column(l, ch):
        buf = gathered.at[l, ch]
        k = l * chains + ch
        own = buf.at[y]
        for d in (2, 1, 3):
            send(own, buf.at[y], f_sem.at[k, 0], f_sem.at[k, 1], y_peer(d))
        for d in (4, 3, 5, 2, 6):
            send(own, buf.at[(DEEP - d) * WIDE + y], f_sem.at[k, 0], z_sem.at[k, DEEP - d - 2], z_peer(d))

    def relay_column(l, ch):
        buf = gathered.at[l, ch]
        k = l * chains + ch
        wait_for(buf.at[pl.ds(0, 3)], f_sem.at[k, 1])
        here = buf.at[pl.ds(0, WIDE)]
        send(here, buf.at[pl.ds(7 * WIDE, WIDE)], f_sem.at[k, 0], f_sem.at[k, 2], z_peer(1))
        send(here, buf.at[pl.ds(WIDE, WIDE)], f_sem.at[k, 0], f_sem.at[k, 2], z_peer(7))
        for zr in (2, 6, 3, 5, 4):
            wait_for(buf.at[pl.ds(0, 1)], z_sem.at[k, zr - 2])
            got = buf.at[zr * WIDE + y]
            for d in (2, 1, 3):
                send(got, got, f_sem.at[k, 0], f_sem.at[k, 2], y_peer(d))

    def forward_term(l, h, rows, t):
        def slot(i):
            column = src[l, i, h, t]
            return (((column >> 2) + (DEEP - z)) & (DEEP - 1)) * WIDE + (column & (WIDE - 1))

        xs = jnp.concatenate([held[slot(i), rows] for i in range(PER)], axis=1)
        ws = jnp.concatenate([blk[l, h * HALF + t * PER + i] for i in range(PER)], axis=1)
        return dot_nt(xs, ws)

    def near_forward(l, ch):
        k = l * chains + ch
        wait_for(gathered.at[l, ch, pl.ds(0, 23)], f_sem.at[k, 2])
        held[:, part(ch)] = gathered[l, ch]

        @pl.when(l == 2)
        def _():
            def step(t, carry):
                pending[2, t, part(ch)] = pending[2, t, part(ch)] + forward_term(l, 1, part(ch), t)
                return carry

            lax.fori_loop(0, ROWS, step, 0, unroll=True)

        def step(t, carry):
            value = forward_term(l, 0, part(ch), t) + pending[l, t, part(ch)]
            part_out[l, ch, t] = value.astype(BF16)
            return carry

        lax.fori_loop(0, ROWS, step, 0, unroll=True)
        for d in (4, 5, 3, 2, 6, 7, 1):
            t = lax.rem(r + d, ROWS)
            send(part_out.at[l, ch, t], part_in.at[l, ch, d - 1], f_sem.at[k, 3], f_sem.at[k, 4], row_peer(d))

    def far_forward(l, rows):
        @pl.when(l < 2)
        def _():
            def step(t, carry):
                pending[lax.rem(l + 1, LOWER), t, rows] = forward_term(l, 1, rows, t)
                return carry

            lax.fori_loop(0, ROWS, step, 0, unroll=True)

    def spread_row(level, ch, value):
        below = lax.rem(level + 2, LOWER)
        buf = copies.at[below, ch]
        k = below * chains + ch
        copies[below, ch, r] = value
        for d in (4, 5, 3, 2, 6, 7, 1):
            send(buf.at[r], buf.at[r], b_sem.at[k, 0], b_sem.at[k, 1], row_peer(d))

    def next_forward(l, ch):
        k = l * chains + ch
        level = l + 1
        wait_for(part_in.at[l, ch], f_sem.at[k, 4])
        update = part_out[l, ch, r].astype(F32)
        for i in range(7):
            update = update + part_in[l, ch, i].astype(F32)
        solved = solve(level, ch, rs_t[level, part(ch)] - update)

        @pl.when(level < LOWER)
        def _():
            gathered[lax.rem(level, LOWER), ch, y] = solved
            spread_column(lax.rem(level, LOWER), ch)

        @pl.when(level == LOWER)
        def _():
            back = dot_nn(solved, inv[LOWER])
            back_t[LOWER, part(ch)] = back
            spread_row(LOWER, ch, back.astype(BF16))

    def scan(l, h, out, rows, count):
        lh = l * 2 + h

        def step(i, total):
            value = held_back[ints[1, lh, i], rows]
            total = total * floats[0, lh, i] + dot_nn(value, blk[l, ints[0, lh, i]])
            out[i, rows] = total
            return total

        lax.fori_loop(0, HALF, step, jnp.zeros((count, N), F32), unroll=True)

    def near_backward(l, ch):
        k = l * chains + ch
        wait_for(copies.at[l, ch, pl.ds(0, 7)], b_sem.at[k, 1])
        held_back[:, part(ch)] = copies[l, ch]

        @pl.when(l == 2)
        def _():
            scan(l, 1, far_scan, part(ch), span)

        scan(l, 0, near_scan, part(ch), span)
        near, far = l * 2, l * 2 + 1

        def step(i, carry):
            for w in range(WIDE):
                j = i * WIDE + w
                value = near_scan[ints[2, near, j], part(ch)] * floats[1, near, j]
                value = value + far_scan[ints[2, far, j], part(ch)] * floats[1, far, j]
                seg[l, ch, i, w] = value.astype(BF16)
            return carry

        lax.fori_loop(0, DEEP, step, 0, unroll=2)
        for d in (2, 1, 3):
            send(seg.at[l, ch, pl.ds(2, 5), lax.rem(y + d, WIDE)], ry.at[l, ch, d - 1],
                 b_sem.at[k, 2], b_sem.at[k, 3], y_peer(d))
        send(seg.at[l, ch, 1], rz.at[l, ch, 0], b_sem.at[k, 2], b_sem.at[k, 4], z_peer(1))
        send(seg.at[l, ch, 7], rz.at[l, ch, 1], b_sem.at[k, 2], b_sem.at[k, 4], z_peer(7))

    def relay_backward(l, ch):
        k = l * chains + ch
        wait_for(ry.at[l, ch], b_sem.at[k, 3])
        for i in (2, 1, 3, 0, 4):
            value = seg[l, ch, i + 2, y].astype(F32)
            for d in range(3):
                value = value + ry[l, ch, d, i].astype(F32)
            s2[l, ch, i] = value.astype(BF16)
            send(s2.at[l, ch, i], fz.at[l, ch, i], b_sem.at[k, 2], b_sem.at[k, 5], z_peer(i + 2))
        wait_for(rz.at[l, ch], b_sem.at[k, 4])
        for d in (2, 1, 3):
            other = lax.rem(y + d, WIDE)
            value = seg[l, ch, 0, other].astype(F32)
            for e in range(2):
                value = value + rz[l, ch, e, other].astype(F32)
            s3[l, ch, d - 1] = value.astype(BF16)
            send(s3.at[l, ch, d - 1], fy.at[l, ch, d - 1], b_sem.at[k, 2], b_sem.at[k, 6], y_peer(d))

    def next_backward(l, ch):
        k = l * chains + ch
        update = seg[l, ch, 0, y].astype(F32)
        for e in range(2):
            update = update + rz[l, ch, e, y].astype(F32)
        wait_for(fy.at[l, ch], b_sem.at[k, 6])
        for i in range(3):
            update = update + fy[l, ch, i].astype(F32)
        wait_for(fz.at[l, ch], b_sem.at[k, 5])
        for i in range(5):
            update = update + fz[l, ch, i].astype(F32)
        rhs = (sol_t[l, part(ch)] - update).astype(BF16)
        back = dot_nn(rhs, inv[l])
        back_t[l, part(ch)] = back

        @pl.when(l > 0)
        def _():
            spread_row(l, ch, back.astype(BF16))

    @functools.partial(each, chains)
    def _(ch):
        gathered[0, ch, y] = solve(0, ch, rs_t[0, part(ch)])

    pl.semaphore_wait(barrier, 17)
    early(lambda ch: spread_column(0, ch))
    index_tables(src, z, int_vec, float_vec)
    move_ints = pltpu.make_async_copy(int_vec, ints, in_sem.at[2 + LOWER])
    move_floats = pltpu.make_async_copy(float_vec, floats, in_sem.at[3 + LOWER])
    move_ints.start()
    move_floats.start()

    @functools.partial(each, LOWER)
    def _(i):
        rs_t[i + 1] = rs[i + 1].T

    move_ints.wait()
    move_floats.wait()

    def far_backward(l, rows):
        @pl.when(l > 0)
        def _():
            scan(lax.rem(l + 2, LOWER), 1, far_scan, rows, half * span)

    @functools.partial(each, LOWER)
    def _(l):
        early(lambda ch: relay_column(l, ch))

        @pl.when(l == 0)
        def _():
            late(lambda ch: spread_column(0, ch))

        @pl.when(l > 0)
        def _():
            late(lambda ch: next_forward(lax.rem(l + 2, LOWER), ch))

        load_blk(l).wait()
        early(lambda ch: near_forward(l, ch))
        late(lambda ch: relay_column(l, ch))
        far_forward(l, early_rows)
        early(lambda ch: next_forward(l, ch))
        late(lambda ch: near_forward(l, ch))
        far_forward(l, late_rows)

    @functools.partial(each, LOWER)
    def _(step):
        l = 2 - step
        early(lambda ch: near_backward(l, ch))

        @pl.when(l == 2)
        def _():
            late(lambda ch: next_forward(2, ch))

        @pl.when(l < 2)
        def _():
            late(lambda ch: next_backward(lax.rem(l + 1, LOWER), ch))

        early(lambda ch: relay_backward(l, ch))
        late(lambda ch: near_backward(l, ch))
        far_backward(l, early_rows)
        early(lambda ch: next_backward(l, ch))
        late(lambda ch: relay_backward(l, ch))
        far_backward(l, late_rows)

    late(lambda ch: next_backward(0, ch))

    @functools.partial(each, LOWER * chains)
    def _(k):
        l, ch = lax.div(k, chains), lax.rem(k, chains)
        wait_for(gathered.at[l, ch, pl.ds(0, 31)], f_sem.at[k, 0])
        wait_for(part_in.at[l, ch], f_sem.at[k, 3])
        wait_for(copies.at[l, ch, pl.ds(0, 7)], b_sem.at[k, 0])
        wait_for(gathered.at[l, ch, pl.ds(0, 31)], b_sem.at[k, 2])


def turn(sol_t, back_t, sol_out, back_out):
    for level in range(LEVELS):
        sol_out[level] = sol_t[level].T.astype(BF16)
        back_out[level] = back_t[level].T


def body(right_sides, inverses, blocks, sources):
    chains = CHAINS
    span = N // chains

    def tile(*lead):
        return pltpu.VMEM((LOWER, chains, *lead, span, N), BF16)

    def whole(*lead, dtype=F32):
        return pltpu.VMEM((*lead, N, N), dtype)

    scratch = [
        whole(LEVELS), whole(LEVELS, dtype=BF16), whole(LEVELS),
        whole(LOWER, 2 * HALF, dtype=BF16),
        tile(COLS), tile(ROWS), tile(ROWS - 1), tile(ROWS),
        tile(DEEP, WIDE), tile(3, 5), tile(2, WIDE), tile(5), tile(3), tile(5), tile(3),
        whole(LOWER, ROWS), whole(COLS, dtype=BF16), whole(ROWS, dtype=BF16), whole(HALF), whole(HALF),
        pltpu.VMEM((3, 8, N), jnp.int32), pltpu.VMEM((2, 8, N), F32),
        pltpu.SMEM((3, 8, N), jnp.int32), pltpu.SMEM((2, 8, N), F32),
        pltpu.SemaphoreType.DMA((4 + LOWER,)),
        pltpu.SemaphoreType.DMA((LOWER * chains, 5)),
        pltpu.SemaphoreType.DMA((LOWER * chains, 5)),
        pltpu.SemaphoreType.DMA((LOWER * chains, 7)),
    ]
    smem = pl.BlockSpec(memory_space=pltpu.SMEM)
    vmem = pl.BlockSpec(memory_space=pltpu.VMEM)
    hbm = pl.BlockSpec(memory_space=pl.ANY)

    def run(*refs):
        kernel(span, *refs)

    solved, back = pl.pallas_call(
        run,
        out_shape=(
            jax.ShapeDtypeStruct((LEVELS, N, N), F32),
            jax.ShapeDtypeStruct((LEVELS, N, N), F32),
        ),
        in_specs=[smem] + [hbm] * 3,
        out_specs=(vmem, vmem),
        scratch_shapes=scratch,
        compiler_params=pltpu.CompilerParams(
            collective_id=0, has_side_effects=True, vmem_limit_bytes=60 * 1024 * 1024
        ),
    )(jnp.transpose(sources[:, 0, 0], (0, 3, 1, 2)), right_sides[:, 0, 0], inverses[:, 0, 0],
      blocks[:, 0, 0].reshape(LOWER, 2 * HALF, N, N))
    solved, back = pl.pallas_call(
        turn,
        out_shape=(
            jax.ShapeDtypeStruct((LEVELS, N, N), BF16),
            jax.ShapeDtypeStruct((LEVELS, N, N), F32),
        ),
        in_specs=[vmem, vmem],
        out_specs=(vmem, vmem),
    )(solved, back)
    return solved[:, None, None], back[:, None, None]


def solution(mesh):
    return jax.shard_map(
        body,
        mesh=mesh,
        in_specs=(
            P(None, "row", "col", None, None),
            P(None, "row", "col", None, None),
            P(None, "row", "col", None, None, None, None, None),
            P(None, "row", "col", None, None, None),
        ),
        out_specs=(P(None, "row", "col", None, None), P(None, "row", "col", None, None)),
        check_vma=False,
    )
```
